256 devices in a mesh: shard: 64 (over z, x, core), rep: 4 (over y).
Axes of the slice: x: 4, y: 4, z: 8, core: 2. Of those that a mesh axis runs over, the one named last changes fastest.
Arguments:
- embeddings: bfloat16 [409600, 1024], P('shard'), may hold values from -6 to 6
- send_index: int32 [409600], P('shard'), may hold values from 0 to 6399, as said below
- place_index: int32 [409600], P('shard'), may hold values from 0 to 6654, as said below
- slot_cluster: int32 [425984], P('shard'), may hold values from -1 to 1663, as said below
- pair_list: int32 [22528, 2], P(('shard', 'rep')), may hold values from 0 to 25, as said below
Outputs:
- best_cosine: float32 [409600], P('shard')
The draws below stay inside these ranges and needn't reach their ends.
Inputs may be any that keep to these rules, and one draw needn't show every extreme that they name: `send_index`: on each device, the entries o * 100 to (o + 1) * 100 - 1 of its block are the local documents sent to owner o; the device's 64 * 100 entries are a permutation of its 6400 documents, so each device sends exactly 100 documents to each owner. `place_index`: on each owner, the 6400 entries are distinct slots, exactly the slots whose slot_cluster is not -1. `slot_cluster`: an owner's 26 * 256 slots form 26 blocks of 256; it holds two or more clusters, each filling one or more consecutive whole blocks with its members first and 1 to 255 padding slots (-1) at the end of its last block, 256 padding slots in all. Ids of owner o lie in o * 26 to o * 26 + 25. `pair_list`: row (o * 4 + r) * 88 + p holds a pair (i, j), i <= j, of blocks of owner o that belong to one cluster; over its 352 rows, owner o lists every such pair at least once, some of them more than once.
All inputs are finite; a program needn't handle non-finite values.
Results may differ from the reference program's by a relative error of at most 0.0014.
Values may be sent and summed in bfloat16 or wider, within the bound.
A program may use at most 128 MiB of HBM per device.

```python
import jax
import jax.numpy as jnp
import numpy as np
from jax import lax

D = 1024
BLK = 256
NB = 26
DOC_DEV = 6400
PAIRS = 88
DOCS = 409600
N_SHARD = 64
N_REP = 4


def owner_layout(key):

    def single(owner_key):
        keys = jax.random.split(owner_key, 3)
        count = jax.random.randint(keys[0], (), 2, NB + 1).astype(jnp.int32)
        lanes = jnp.arange(NB - 1, dtype=jnp.int32)
        block_perm = jax.random.permutation(keys[1], NB - 1).astype(jnp.int32) + 1
        block_cuts = jnp.sort(jnp.where(lanes < count - 1, block_perm, NB))
        pad_perm = jax.random.permutation(keys[2], BLK - 2)[:NB - 1].astype(jnp.int32) + 1
        pad_perm = pad_perm.at[0].set(BLK - 1)
        pad_cuts = jnp.sort(jnp.where(lanes < count - 1, pad_perm, BLK))
        zero = jnp.zeros((1,), jnp.int32)
        edges = jnp.concatenate([zero, block_cuts, jnp.full((1,), NB, jnp.int32)])
        padding = jnp.diff(jnp.concatenate([zero, pad_cuts, jnp.full((1,), BLK, jnp.int32)]))
        block_ids = jnp.arange(NB, dtype=jnp.int32)
        cluster_of_block = jnp.sum((block_cuts[None, :] <= block_ids[:, None]).astype(jnp.int32), axis=1)
        last_block = edges[1:] - 1
        is_last = last_block[cluster_of_block] == block_ids
        pad_here = padding[cluster_of_block]
        position = jnp.arange(BLK, dtype=jnp.int32)
        live = ~(is_last[:, None] & (position[None, :] >= BLK - pad_here[:, None]))
        return (cluster_of_block, live.reshape(-1))
    return jax.vmap(single)(jax.random.split(key, N_SHARD))


def draw_send_index(key, part):
    key = jax.random.fold_in(key, 5)
    keys = jax.random.split(key, N_SHARD)
    orders = jax.vmap(lambda k: jax.random.permutation(k, DOC_DEV).astype(jnp.int32))(keys)
    return orders.reshape(-1)


def draw_slot_cluster(key, part):
    cluster_of_block, live = owner_layout(key)
    lift = NB - 1 - jnp.max(cluster_of_block, axis=1, keepdims=True)
    ids = jnp.arange(N_SHARD, dtype=jnp.int32)[:, None] * NB + cluster_of_block + lift
    spread = jnp.repeat(ids, BLK, axis=1)
    return jnp.where(live, spread, -1).astype(jnp.int32).reshape(-1)


def draw_place_index(key, part):
    cluster_of_block, live = owner_layout(key)
    key = jax.random.fold_in(key, 9)
    order = jnp.argsort(1 - live.astype(jnp.int32), axis=1, stable=True).astype(jnp.int32)[:, :DOC_DEV]
    keys = jax.random.split(key, N_SHARD)
    shuffles = jax.vmap(lambda k: jax.random.permutation(k, DOC_DEV).astype(jnp.int32))(keys)
    return jnp.take_along_axis(order, shuffles, axis=1).reshape(-1)


def draw_pair_list(key, part):
    cluster_of_block, live = owner_layout(key)
    upper = np.triu_indices(NB)
    first = jnp.asarray(upper[0], dtype=jnp.int32)
    second = jnp.asarray(upper[1], dtype=jnp.int32)
    valid = (cluster_of_block[:, first] == cluster_of_block[:, second]).astype(jnp.int32)
    order = jnp.argsort(1 - valid, axis=1, stable=True).astype(jnp.int32)
    total = jnp.sum(valid, axis=1).astype(jnp.int32)
    rank = jnp.arange(N_REP, dtype=jnp.int32)
    held = (total[:, None] - rank[None, :] + N_REP - 1) // N_REP
    row = jnp.arange(PAIRS, dtype=jnp.int32)
    picks = rank[None, :, None] + N_REP * (row[None, None, :] % held[:, :, None])
    picks = picks.reshape(N_SHARD, N_REP * PAIRS).astype(jnp.int32)
    chosen = jnp.take_along_axis(order, picks, axis=1)
    pairs = jnp.stack([first[chosen], second[chosen]], axis=-1)
    return pairs.reshape(-1, 2).astype(jnp.int32)


def shard_levels(stream_key, shape, cuts, least, top_value):
    def one(dim, shards_of):
        heights = jax.random.uniform(jax.random.fold_in(jax.random.fold_in(stream_key, 6), dim), (shards_of,), jnp.float32, least / len(cuts), top_value / len(cuts))
        return jnp.repeat(jnp.exp(heights), shape[dim] // shards_of).reshape((-1,) + (1,) * (len(shape) - dim - 1))

    loudness = one(*cuts[0])
    for cut in cuts[1:]:
        loudness = loudness * one(*cut)
    return loudness


def scatter_about(key, shape, scale, limit, cuts=(), kind=jnp.bfloat16):
    entries = scale * jax.random.normal(key, shape, jnp.float32)
    if cuts:
        entries = entries * shard_levels(key, shape, cuts, -0.22, 0.18)
    return jnp.clip(entries, -limit, limit).astype(kind)


def setup_inputs(seed: int = 0) -> dict:
    seeds = jax.random.split(jax.random.key(seed), 6)
    embeddings = scatter_about(seeds[0], (DOCS, D), 1.0, 6.0, ((0, 64),))
    send_index = draw_send_index(jax.random.fold_in(seeds[5], 71), 0)
    place_index = draw_place_index(jax.random.fold_in(seeds[5], 71), 0)
    slot_cluster = draw_slot_cluster(jax.random.fold_in(seeds[5], 71), 0)
    pair_list = draw_pair_list(jax.random.fold_in(seeds[5], 71), 0)
    return dict(embeddings=embeddings, send_index=send_index, place_index=place_index, slot_cluster=slot_cluster, pair_list=pair_list)


def reference(embeddings, send_index, place_index, slot_cluster, pair_list):
    wide = embeddings.astype(jnp.float32)
    normed = (wide * lax.rsqrt(lax.optimization_barrier(jnp.sum(wide * wide, axis=1, keepdims=True)) + 1e-06)).astype(jnp.bfloat16)
    share = DOC_DEV // N_SHARD
    sends = send_index.reshape(N_SHARD, N_SHARD, share)
    offsets = (jnp.arange(N_SHARD, dtype=jnp.int32) * DOC_DEV)[None, :, None]
    documents = jnp.transpose(sends, (1, 0, 2)) + offsets
    places = place_index.reshape(N_SHARD, N_SHARD * share)
    clusters = slot_cluster.reshape(N_SHARD, NB, BLK)
    pairs = pair_list.reshape(N_SHARD, N_REP * PAIRS, 2)
    diagonal = jnp.eye(BLK, dtype=bool)

    def owner(items):
        doc_owner, place_owner, cluster_owner, pair_owner = items
        slot_doc = jnp.zeros((NB * BLK,), jnp.int32).at[place_owner].set(doc_owner.reshape(-1))
        blocks = normed[slot_doc].reshape(NB, BLK, D)
        count = pair_owner.shape[0]
        same = (pair_owner[:, None, 0] == pair_owner[None, :, 0]) & (pair_owner[:, None, 1] == pair_owner[None, :, 1])
        earlier = jnp.arange(count)[None, :] < jnp.arange(count)[:, None]
        repeat = jnp.any(same & earlier, axis=1)

        def visit(best, item):
            pair, again = item

            def fresh(current):
                first = pair[0]
                second = pair[1]
                gram = jnp.dot(blocks[first], blocks[second].T, preferred_element_type=jnp.float32)
                left = cluster_owner[first]
                right = cluster_owner[second]
                counts = (left[:, None] == right[None, :]) & (left[:, None] >= 0)
                counts = counts & ~((first == second) & diagonal)
                values = jnp.where(counts, gram, jnp.float32(-1.0))
                current = current.at[first].max(lax.optimization_barrier(jnp.max(values, axis=1)))
                return current.at[second].max(lax.optimization_barrier(jnp.max(values, axis=0)))
            return (lax.cond(again, lambda current: current, fresh, best), None)
        start = jnp.full((NB, BLK), -1.0, jnp.float32)
        best = lax.scan(visit, start, (pair_owner, repeat))[0]
        return best.reshape(-1)[place_owner]
    values = lax.map(owner, (documents, places, clusters, pairs))
    return jnp.zeros((N_SHARD * DOC_DEV,), jnp.float32).at[documents.reshape(-1)].set(values.reshape(-1))
```

```python
import functools

import jax
import jax.numpy as jnp
from jax import lax
from jax.experimental import pallas as pl
from jax.experimental.pallas import tpu as pltpu
from jax.sharding import PartitionSpec as P

D = 1024
BLK = 256
DOCS = 6400
NS = 64
NR = 4
SHARE = 100
PART = 25
PADDED = 26
MSG = PADDED * 8
GROUP = PADDED * 8
NG = 8
CHUNK = 400
NCHUNK = DOCS // CHUNK
STG = 0
CS = 2048
RA = 8192
MESH = pl.DeviceIdType.MESH
F32 = jnp.float32
BF16 = jnp.bfloat16
LAST = (((1,), (1,)), ((), ()))


def pieces(v):
    a = v.astype(BF16).astype(F32)
    r = v - a
    b = r.astype(BF16).astype(F32)
    return a, b, r - b


def kernel(
    send_ref, table_ref, emb_ref, idx_ref, place_ref, out_ref,
    wide, q, outb, recv, emb, colacc, cl, ctmp, lhs, rhs, tsrc, trecv, trow, vrecv,
    esem, zsend, zrecv, ysend, yrecv, r1send, r1recv, r2send, r2recv,
):
    me = lax.axis_index("shard")
    rep = lax.axis_index("rep")
    z, x, c = me // 8, (me // 2) % 4, me % 2
    role = jnp.where(c == 0, rep, 3 - rep)
    odd = role % 2

    def rep_of(r):
        r = (r + 4) % 4
        return jnp.where(c == 0, r, 3 - r)

    own_pos = jnp.where(role == 3, 1, 0)
    first_pos = jnp.where(role == 0, 0, 1)
    second_to = jnp.where(role == 2, rep_of(3), rep_of(1))
    y0 = jnp.where(role == 3, rep_of(0), rep_of(role))
    y1 = jnp.where(role == 3, rep_of(3), rep_of(role + 1))
    y2 = jnp.where(role == 1, rep_of(3), jnp.where(role == 3, rep_of(2), -1))

    def fetch(ch, slot):
        return pltpu.make_async_copy(
            emb_ref.at[pl.ds(pl.multiple_of(ch * CHUNK, 16), CHUNK)], emb.at[slot], esem.at[slot]
        )

    fetch(0, 0).start()
    fetch(1, 1).start()

    barrier = pltpu.get_barrier_semaphore()

    @pl.loop(1, NS)
    def _(k):
        pl.semaphore_signal(barrier, inc=1, device_id={"shard": (me + k) % NS}, device_id_type=MESH)

    for k in range(1, NR):
        pl.semaphore_signal(barrier, inc=1, device_id={"rep": (rep + k) % NR}, device_id_type=MESH)

    @pl.loop(0, NCHUNK)
    def _(ch):
        slot = ch % 2
        fetch(ch, slot).wait()

        @pl.loop(0, CHUNK // 16, unroll=5)
        def _(r):
            rows = emb[slot, pl.ds(pl.multiple_of(r * 16, 16), 16), :].astype(F32)
            base = ch * (CHUNK * 8) + r * 128
            for h in range(2):
                for j in range(8):
                    wide[pl.ds(pl.multiple_of(base + h * 64 + j * 8, 8), 8), :] = rows[
                        8 * h : 8 * h + 8, 128 * j : 128 * j + 128
                    ]

        @pl.when(ch + 2 < NCHUNK)
        def _():
            fetch(ch + 2, slot).start()

    pl.semaphore_wait(barrier, NS - 1 + NR - 1)

    def zcopy(dst):
        return pltpu.make_async_remote_copy(
            src_ref=outb.at[dst], dst_ref=recv.at[me], send_sem=zsend.at[dst], recv_sem=zrecv.at[me],
            device_id={"shard": dst}, device_id_type=MESH,
        )

    def zlocal():
        return pltpu.make_async_copy(outb.at[me], recv.at[me], zrecv.at[me])

    def address(i):
        return (i // 8) * 64 + i % 8

    @pl.loop(0, NS)
    def _(k):
        t, h, w, b = k // 16, (k // 8) % 2, (k // 2) % 4, k % 2
        dst = ((z + h + 2 * w) % 8) * 8 + ((x + t) % 4) * 2 + (c + b) % 2
        base = dst * SHARE + rep * PART
        for a in range(PADDED // 2):
            i0 = send_ref[base + 2 * a]
            i1 = send_ref[base + min(2 * a + 1, PART - 1)]
            v0 = wide[pl.ds(address(i0), 8, stride=8), :]
            v1 = wide[pl.ds(address(i1), 8, stride=8), :]
            outb[dst, pl.ds(16 * a, 16), :] = jnp.concatenate([v0, v1], axis=0).astype(BF16)

        @pl.when(dst != me)
        def _():
            zcopy(dst).start()

        @pl.when(dst == me)
        def _():
            zlocal().start()

    place = place_ref[...]
    block = place // BLK
    ids = jnp.full((NS, 128), -1.0, F32)
    for b in range(table_ref.shape[0] // BLK):
        ids = jnp.where(block == b, (table_ref[b * BLK] - me * 26).astype(F32), ids)
    ids = jnp.where(place >= 0, ids, -1.0)
    ctmp[...] = ids
    for g in range(NG):
        for e in range(8):
            s = ((e // 2) * 2 + g % 2) * 8 + (g // 2) * 2 + e % 2
            tsrc[8 * g + e : 8 * g + e + 1, :] = ctmp[s : s + 1, :]
    ordered = tsrc[...].astype(BF16)
    lane = lax.broadcasted_iota(jnp.int32, (128, 256), 0)
    spot = lax.broadcasted_iota(jnp.int32, (128, 256), 1)
    keep = (lax.broadcasted_iota(jnp.int32, (NS, 256), 1) % 8) == (
        lax.broadcasted_iota(jnp.int32, (NS, 256), 0) % 8
    )
    for y in range(NR):
        spread = (lane == 32 * y + spot // 8).astype(F32).astype(BF16)
        ids_y = jnp.dot(ordered, spread, preferred_element_type=F32)
        ids_y = jnp.where(keep, ids_y, 0.0)
        for g in range(NG):
            row = jnp.sum(ids_y[8 * g : 8 * g + 8, :], axis=0, keepdims=True)
            cl[y * NG + g] = jnp.broadcast_to(row, (8, 256))

    @pl.loop(0, 2 * NG)
    def _(k):
        y = jnp.where(k // NG == 0, y0, y1)
        rows = cl[y * NG + k % NG]
        for h in range(2):
            tile = jnp.broadcast_to(rows[0:1, 128 * h : 128 * h + 128], (128, 128))
            wide[pl.ds(pl.multiple_of(CS + k * 256 + h * 128, 8), 128), :] = tile.T

    wide[RA : RA + 2 * NG * GROUP, :] = jnp.full((2 * NG * GROUP, 128), -1.0, F32)
    colacc[...] = jnp.full(colacc.shape, -1.0, F32)

    @pl.loop(0, 3 * NG)
    def _(k):
        q[k // NG, k % NG, GROUP:256, :] = jnp.zeros((256 - GROUP, D), BF16)

    sub = lax.broadcasted_iota(jnp.int32, (128, 128), 0)
    low = idx_ref[...]
    low = jnp.where(low >= 0, low % 128, -1)
    for o in range(NS):
        rhs[:, 128 * o : 128 * o + 128] = (sub == low[o : o + 1, :]).astype(F32).astype(BF16)

    def group_of(n):
        return ((x - n // 2 + 4) % 4) * 2 + (z + n) % 2

    def ycopy(n, which):
        g = group_of(n)
        pos = first_pos if which == 0 else 2
        dev = rep_of(role - 1) if which == 0 else second_to
        return pltpu.make_async_remote_copy(
            src_ref=q.at[own_pos, g, pl.ds(0, GROUP)], dst_ref=q.at[pos, g, pl.ds(0, GROUP)],
            send_sem=ysend.at[which, n], recv_sem=yrecv.at[which, n],
            device_id={"rep": dev}, device_id_type=MESH,
        )

    def arrive(n):
        g = group_of(n)
        xs, zs = g // 2, g % 2

        @pl.loop(0, 8)
        def _(e):
            s = ((e // 2) * 2 + zs) * 8 + xs * 2 + e % 2

            @pl.when(s != me)
            def _():
                pltpu.make_async_remote_copy(
                    src_ref=outb.at[s], dst_ref=recv.at[s], send_sem=zsend.at[s], recv_sem=zrecv.at[s],
                    device_id={"shard": s}, device_id_type=MESH,
                ).wait_recv()

            @pl.when(s == me)
            def _():
                zlocal().wait()

            docs = recv[s].astype(F32)
            for i in range(PADDED):
                wide[pl.ds(STG + i * 64 + e, 8, stride=8), :] = docs[8 * i : 8 * i + 8, :]

        @pl.loop(0, GROUP // 16)
        def _(a):
            v = wide[pl.ds(pl.multiple_of(STG + a * 128, 8), 128), :]
            part = []
            for h in range(2):
                tiles = [v[64 * h + 8 * j : 64 * h + 8 * j + 8, :] for j in range(8)]
                square = tiles[0] * tiles[0]
                for j in range(1, 8):
                    square = square + tiles[j] * tiles[j]
                scale = lax.rsqrt(jnp.sum(square, axis=1, keepdims=True) + 1e-06)
                part.append([tile * scale for tile in tiles])
            for j in range(8):
                q[own_pos, g, pl.ds(pl.multiple_of(a * 16, 16), 16), 128 * j : 128 * j + 128] = jnp.concatenate(
                    [part[0][j], part[1][j]], axis=0
                ).astype(BF16)

        ycopy(n, 0).start()

        @pl.when(role >= 2)
        def _():
            ycopy(n, 1).start()

    away = lax.broadcasted_iota(jnp.int32, (GROUP, 256), 0) - lax.broadcasted_iota(jnp.int32, (GROUP, 256), 1)

    def tile(pa, ga, pb, gb, diagonal):
        g = lax.dot_general(q[pa, ga, 0:GROUP, :], q[pb, gb], LAST, preferred_element_type=F32)
        yb = jnp.where(pb == 0, y0, jnp.where(pb == 1, y1, y2))
        left = wide[pl.ds(pl.multiple_of(CS + (pa * NG + ga) * 256, 8), GROUP), :]
        right = cl[yb * NG + gb]
        at = pl.multiple_of(RA + (pa * NG + ga) * GROUP, 8)
        rows = wide[pl.ds(at, GROUP), :]
        for h in range(2):
            same = left.reshape(PADDED, 8, 128) == right[None, :, 128 * h : 128 * h + 128]
            if diagonal is not None:
                away_h = away[:, 128 * h : 128 * h + 128].reshape(PADDED, 8, 128)
                same = same & (away_h != jnp.where(diagonal, 0, 4096))
            vals = jnp.where(same, g[:, 128 * h : 128 * h + 128].reshape(PADDED, 8, 128), -1.0)
            rows = jnp.maximum(rows, vals.reshape(GROUP, 128))
            at_c = pb * NG + gb
            colacc[at_c, :, 128 * h : 128 * h + 128] = jnp.maximum(
                colacc[at_c, :, 128 * h : 128 * h + 128], jnp.max(vals, axis=0)
            )
        wide[pl.ds(at, GROUP), :] = rows

    def score(n):
        g = group_of(n)
        ycopy(n, 0).wait_recv()

        @pl.when(odd == 1)
        def _():
            ycopy(n, 1).wait_recv()

        @pl.loop(0, n)
        def _(m):
            gm = group_of(m)
            for v in range(4):
                ga = jnp.where((odd == 1) & (v >= 2), gm, g)
                gb = jnp.where((odd == 1) & (v >= 2), g, gm)
                pa = jnp.where(odd == 1, 0, v // 2)
                pb = jnp.where(odd == 1, 1 + v % 2, v % 2)
                tile(pa, ga, pb, gb, None)

        tile(0, g, 1, g, None)
        tile(0, g, jnp.where(odd == 1, 2, 0), g, odd == 0)

        @pl.when(odd == 0)
        def _():
            tile(1, g, 1, g, True)

    @pl.loop(0, NG + 1)
    def _(n):
        @pl.when(n < NG)
        def _():
            arrive(n)

        @pl.when(n > 0)
        def _():
            score(n - 1)

    spot8 = lax.broadcasted_iota(jnp.int32, (8, 256), 1) % 8 == lax.broadcasted_iota(jnp.int32, (8, 256), 0)
    out_lane = lax.broadcasted_iota(jnp.int32, (256, 128), 1) % 32
    gather = (lax.broadcasted_iota(jnp.int32, (256, 128), 0) // 8 == out_lane).astype(F32).astype(BF16)
    lane8 = lax.broadcasted_iota(jnp.int32, (8, 128), 1)
    tsrc[...] = jnp.full(tsrc.shape, -1.0, F32)

    @pl.loop(0, 3)
    def _(p):
        yp = jnp.where(p == 0, y0, jnp.where(p == 1, y1, y2))
        parts = ([], [], [])
        for g in range(NG):
            col = jnp.max(colacc[p * NG + g], axis=0, keepdims=True)
            for part, kept in zip(parts, pieces(col)):
                part.append(jnp.where(spot8, kept, 0.0).astype(BF16).astype(F32))
        best = 0.0
        for part in parts:
            left = jnp.concatenate(part, axis=0).astype(BF16)
            best = best + jnp.dot(left, gather, preferred_element_type=F32)
        mine = lax.broadcasted_iota(jnp.int32, (NS, 128), 1) // 32 == yp
        tsrc[...] = jnp.maximum(tsrc[...], jnp.where(mine, best, -1.0))

    @pl.loop(0, 2 * NG)
    def _(k):
        yp = jnp.where(k // NG == 0, y0, y1)
        rows = wide[pl.ds(pl.multiple_of(RA + k * GROUP, 8), GROUP), :].reshape(PADDED, 8, 128)
        rows = jnp.max(rows, axis=2, keepdims=True)
        best = jnp.full((8, 128), -1.0, F32)
        for i in range(PADDED):
            best = jnp.where(lane8 % 32 == i, rows[i], best)
        at = pl.ds(pl.multiple_of((k % NG) * 8, 8), 8)
        tsrc[at, :] = jnp.maximum(tsrc[at, :], jnp.where(lane8 // 32 == yp, best, -1.0))

    def r1(k):
        dev = (rep + k) % NR
        return pltpu.make_async_remote_copy(
            src_ref=tsrc, dst_ref=trecv.at[k], send_sem=r1send.at[k], recv_sem=r1recv.at[k],
            device_id={"rep": dev}, device_id_type=MESH,
        )

    for k in range(1, NR):
        r1(k).start()
    for k in range(1, NR):
        r1(k).wait_recv()
    full = jnp.maximum(jnp.maximum(tsrc[...], trecv[1]), jnp.maximum(trecv[2], trecv[3]))
    for r in range(NS):
        trow[r] = full[r : r + 1, :]

    def slot_of(s):
        zz, xx, cc = s // 8, (s // 2) % 4, s % 2
        return (xx * 2 + zz % 2) * 8 + (zz // 2) * 2 + cc

    def r2(s):
        return pltpu.make_async_remote_copy(
            src_ref=trow.at[slot_of(s)], dst_ref=vrecv.at[me], send_sem=r2send.at[s], recv_sem=r2recv.at[me],
            device_id={"shard": s}, device_id_type=MESH,
        )

    @pl.loop(1, NS)
    def _(k):
        r2((me + k) % NS).start()

    vrecv[me] = trow[slot_of(me)]

    @pl.loop(1, NS)
    def _(k):
        s = (me + k) % NS
        pltpu.make_async_remote_copy(
            src_ref=trow.at[slot_of(s)], dst_ref=vrecv.at[s], send_sem=r2send.at[s], recv_sem=r2recv.at[s],
            device_id={"shard": s}, device_id_type=MESH,
        ).wait_recv()

    sub64 = lax.broadcasted_iota(jnp.int32, (64, 128), 0)
    high = idx_ref[...]
    high = jnp.where(high >= 0, high // 128, -1)
    for o in range(NS):
        hit = sub64 == high[o : o + 1, :]
        for w, kept in enumerate(pieces(vrecv[o])):
            lhs[64 * w : 64 * w + 64, 128 * o : 128 * o + 128] = jnp.where(hit, kept, 0.0).astype(BF16)
    done = lax.dot_general(lhs[...], rhs[...], LAST, preferred_element_type=F32)
    done = done[0:64, :] + done[64:128, :] + done[128:192, :]
    out_ref[...] = done[0 : DOCS // 128, :]

    @pl.loop(1, NS)
    def _(k):
        s = (me + k) % NS
        zcopy(s).wait_send()
        r2(s).wait_send()

    for k in range(1, NR):
        r1(k).wait_send()

    @pl.loop(0, NG)
    def _(n):
        ycopy(n, 0).wait_send()

        @pl.when(role >= 2)
        def _():
            ycopy(n, 1).wait_send()


def shards(embeddings, send_index, place_index, slot_cluster, pair_list):
    def lanes(a):
        a = a.reshape(NS, NR, PART)
        return jnp.pad(a, ((0, 0), (0, 0), (0, 32 - PART)), constant_values=-1).reshape(NS, 128)

    vm = pl.BlockSpec(memory_space=pltpu.VMEM)
    sm = pl.BlockSpec(memory_space=pltpu.SMEM)
    dma = pltpu.SemaphoreType.DMA
    out = pl.pallas_call(
        kernel,
        out_shape=jax.ShapeDtypeStruct((DOCS // 128, 128), F32),
        in_specs=[sm, sm, pl.BlockSpec(memory_space=pl.ANY), vm, vm],
        out_specs=vm,
        scratch_shapes=[
            pltpu.VMEM((DOCS * 8, 128), F32),
            pltpu.VMEM((3, NG, 256, D), BF16),
            pltpu.VMEM((NS, MSG, 128), BF16),
            pltpu.VMEM((NS, MSG, 128), BF16),
            pltpu.VMEM((2, CHUNK, D), BF16),
            pltpu.VMEM((3 * NG, 8, 256), F32),
            pltpu.VMEM((NR * NG, 8, 256), F32),
            pltpu.VMEM((NS, 128), F32),
            pltpu.VMEM((192, NS * 128), BF16),
            pltpu.VMEM((128, NS * 128), BF16),
            pltpu.VMEM((NS, 128), F32),
            pltpu.VMEM((NR, NS, 128), F32),
            pltpu.VMEM((NS, 1, 128), F32),
            pltpu.VMEM((NS, 1, 128), F32),
            dma((2,)),
            dma((NS,)),
            dma((NS,)),
            dma((2, NG)),
            dma((2, NG)),
            dma((NR,)),
            dma((NR,)),
            dma((NS,)),
            dma((NS,)),
        ],
        compiler_params=pltpu.CompilerParams(
            collective_id=0, has_side_effects=True, vmem_limit_bytes=60 * 1024 * 1024
        ),
        name="dedup",
    )(send_index, slot_cluster, embeddings, lanes(send_index), lanes(place_index))
    return out.reshape(-1)


def solution(mesh):
    return jax.shard_map(
        shards,
        mesh=mesh,
        in_specs=(P("shard", None), P("shard"), P("shard"), P("shard"), P(("shard", "rep"), None)),
        out_specs=P("shard"),
        check_vma=False,
    )
```

```python
import functools

import jax
import jax.numpy as jnp
from jax import lax
from jax.experimental import pallas as pl
from jax.experimental.pallas import tpu as pltpu
from jax.sharding import PartitionSpec as P

D = 1024
BLK = 256
DOCS = 6400
NS = 64
NR = 4
SHARE = 100
PART = 25
PADDED = 26
MSG = PADDED * 8
GROUP = PADDED * 8
NG = 8
CHUNK = 400
NCHUNK = DOCS // CHUNK
NBUF = 8
FLAT = DOCS // 128
MESH = pl.DeviceIdType.MESH
F32 = jnp.float32
BF16 = jnp.bfloat16
LAST = (((1,), (1,)), ((), ()))


def pieces(v):
    a = v.astype(BF16).astype(F32)
    r = v - a
    b = r.astype(BF16).astype(F32)
    return a, b, r - b


def kernel(
    send_hbm, table_hbm, emb_ref, idx_hbm, place_hbm, out_ref,
    send_ref, table_ref, idx_ref, place_ref,
    wide, q, outb, recv, emb, stage, cs, ra, colacc, cl, ctmp, tsrc, trecv, trow, vrecv, res,
    isem, bsem, esem, zsend, zrecv, ysend, yrecv, r1send, r1recv, r2send, r2recv, r3send, r3recv,
):
    me = lax.axis_index("shard")
    rep = lax.axis_index("rep")
    z, x, c = me // 8, (me // 2) % 4, me % 2
    def rep_of(r):
        return (r + 2 * c) % 4

    def pick(a, b, c_, d):
        return jnp.where(role == 0, a, jnp.where(role == 1, b, jnp.where(role == 2, c_, d)))

    role = rep_of(rep)
    y0 = rep
    y1 = rep_of(pick(3, 0, 1, 3))
    y2 = rep_of(pick(0, 2, 3, 0))

    def fetch(ch, slot):
        return pltpu.make_async_copy(
            emb_ref.at[pl.ds(pl.multiple_of(ch * CHUNK, 16), CHUNK)], emb.at[slot], esem.at[slot]
        )

    ints = [
        pltpu.make_async_copy(a, b, isem.at[i])
        for i, (a, b) in enumerate(
            [(send_hbm, send_ref), (table_hbm, table_ref), (idx_hbm, idx_ref), (place_hbm, place_ref)]
        )
    ]
    for i in range(NBUF):
        fetch(i, i).start()
    for copy in ints:
        copy.start()

    def in_line(k):
        return {"shard": ((z + k) % 8) * 8 + x * 2 + c}

    def in_plane(k):
        return {"shard": z * 8 + (x * 2 + c + k) % 8}

    barrier = pltpu.get_barrier_semaphore()
    for k in range(1, NR):
        pl.semaphore_signal(barrier, inc=1, device_id={"rep": (rep + k) % NR}, device_id_type=MESH)
    for k in range(1, 8):
        pl.semaphore_signal(barrier, inc=1, device_id=in_plane(k), device_id_type=MESH)
        pl.semaphore_signal(barrier, inc=1, device_id=in_line(k), device_id_type=MESH)

    @pl.loop(0, NCHUNK)
    def _(ch):
        slot = ch % NBUF
        fetch(ch, slot).wait()

        @pl.loop(0, CHUNK // 16, unroll=5)
        def _(r):
            rows = emb[slot, pl.ds(pl.multiple_of(r * 16, 16), 16), :].astype(F32)
            base = ch * (CHUNK * 8) + r * 128
            for h in range(2):
                for j in range(8):
                    wide[pl.ds(pl.multiple_of(base + h * 64 + j * 8, 8), 8), :] = rows[
                        8 * h : 8 * h + 8, 128 * j : 128 * j + 128
                    ]

        @pl.when(ch + NBUF < NCHUNK)
        def _():
            fetch(ch + NBUF, slot).start()

        @pl.when(ch == NCHUNK // 2)
        def _():
            pl.semaphore_wait(barrier, 14 + NR - 1)
            for k in range(1, 8):
                pl.semaphore_signal(bsem, inc=1, device_id=in_plane(k), device_id_type=MESH)

    for copy in ints:
        copy.wait()
    pl.semaphore_wait(bsem, 7)

    def zcopy(dst):
        return pltpu.make_async_remote_copy(
            src_ref=outb.at[dst], dst_ref=recv.at[me], send_sem=zsend.at[dst], recv_sem=zrecv.at[me],
            device_id={"shard": dst}, device_id_type=MESH,
        )

    def zlocal():
        return pltpu.make_async_copy(outb.at[me], recv.at[me], zrecv.at[me])

    def address(i):
        return (i // 8) * 64 + i % 8

    def send(k):
        n = k // 8
        t, h, w, b = n // 2, n % 2, (k // 2) % 4, k % 2
        dst = ((z + h + 2 * w) % 8) * 8 + ((x + t) % 4) * 2 + (c + b) % 2
        base = dst * SHARE + rep * PART
        for a in range(PADDED // 2):
            i0 = send_ref[base + 2 * a]
            i1 = send_ref[base + min(2 * a + 1, PART - 1)]
            v0 = wide[pl.ds(address(i0), 8, stride=8), :]
            v1 = wide[pl.ds(address(i1), 8, stride=8), :]
            outb[dst, pl.ds(16 * a, 16), :] = jnp.concatenate([v0, v1], axis=0).astype(BF16)

        @pl.when(dst != me)
        def _():
            zcopy(dst).start()

        @pl.when(dst == me)
        def _():
            zlocal().start()

    @pl.loop(0, NS)
    def _(k):
        send(k)

    lane1 = lax.broadcasted_iota(jnp.int32, (1, 128), 1)

    def share_of(flat, o):
        a, off = o * SHARE // 128, o * SHARE % 128
        b = min(a + 1, FLAT - 1)
        both = jnp.where(lane1 >= off, flat[a : a + 1, :], flat[b : b + 1, :])
        both = both if off == 0 else pltpu.roll(both, 128 - off, 1)
        return jnp.where(lane1 < SHARE, both, -1)

    for g in range(NG):
        for e in range(8):
            s = ((e // 2) * 2 + g % 2) * 8 + (g // 2) * 2 + e % 2
            ctmp[8 * g + e : 8 * g + e + 1, :] = share_of(place_ref, s)
    block = ctmp[...] // BLK
    ids = jnp.full((NS, 128), -1.0, F32)
    for b in range(table_ref.shape[0] // BLK):
        ids = jnp.where(block == b, (table_ref[b * BLK] - me * 26).astype(F32), ids)
    ordered = ids.astype(BF16)
    lane = lax.broadcasted_iota(jnp.int32, (128, 256), 0)
    spot = lax.broadcasted_iota(jnp.int32, (128, 256), 1)
    keep = (lax.broadcasted_iota(jnp.int32, (NS, 256), 1) % 8) == (
        lax.broadcasted_iota(jnp.int32, (NS, 256), 0) % 8
    )
    for y in range(NR):
        spread = ((lane == PART * y + spot // 8) & (spot < 8 * PART)).astype(F32).astype(BF16)
        ids_y = jnp.dot(ordered, spread, preferred_element_type=F32)
        ids_y = jnp.where(keep, ids_y, 0.0)
        for g in range(NG):
            row = jnp.sum(ids_y[8 * g : 8 * g + 8, :], axis=0, keepdims=True)
            cl[y * NG + g] = jnp.broadcast_to(jnp.where(spot[0:1, :] < 8 * PART, row, -1.0), (8, 256))

    @pl.loop(0, 2 * NG)
    def _(k):
        y = jnp.where(k // NG == 0, y0, y1)
        rows = cl[y * NG + k % NG]
        for h in range(2):
            tile = jnp.broadcast_to(rows[0:1, 128 * h : 128 * h + 128], (128, 128))
            cs[pl.ds(pl.multiple_of(k * 256 + h * 128, 8), 128), :] = tile.T

    ra[...] = jnp.full(ra.shape, -1.0, F32)
    colacc[...] = jnp.full(colacc.shape, -1.0, F32)

    @pl.loop(0, 3 * NG)
    def _(k):
        q[k // NG, k % NG, GROUP:256, :] = jnp.zeros((256 - GROUP, D), BF16)

    sub = lax.broadcasted_iota(jnp.int32, (128, 128), 0)
    for o in range(NS):
        low = share_of(idx_ref, o)
        ctmp[o : o + 1, :] = low
        low = jnp.where(low >= 0, low % 128, -1)
        emb[o // 8, 192:320, 128 * (o % 8) : 128 * (o % 8) + 128] = (sub == low).astype(F32).astype(BF16)

    def group_of(n):
        return ((x - n // 2 + 4) % 4) * 2 + (z + n) % 2

    def ycopy(n, which):
        g = group_of(n)
        at = jnp.where(role >= 2, 1, 0) if which == 0 else 0
        dev = rep_of(pick(1, 2, 1, 2)) if which == 0 else rep_of(0)
        return pltpu.make_async_remote_copy(
            src_ref=q.at[0, g, pl.ds(0, GROUP)], dst_ref=q.at[1 + at, g, pl.ds(0, GROUP)],
            send_sem=ysend.at[which, n], recv_sem=yrecv.at[at, n],
            device_id={"rep": dev}, device_id_type=MESH,
        )

    def ywait(n, at):
        g = group_of(n)
        pltpu.make_async_remote_copy(
            src_ref=q.at[0, g, pl.ds(0, GROUP)], dst_ref=q.at[1 + at, g, pl.ds(0, GROUP)],
            send_sem=ysend.at[0, n], recv_sem=yrecv.at[at, n],
            device_id={"rep": rep_of(pick(1, 2, 1, 2))}, device_id_type=MESH,
        ).wait_recv()

    def arrive(n):
        g = group_of(n)
        xs, zs = g // 2, g % 2

        @pl.loop(0, 8)
        def _(e):
            s = ((e // 2) * 2 + zs) * 8 + xs * 2 + e % 2

            @pl.when(s != me)
            def _():
                pltpu.make_async_remote_copy(
                    src_ref=outb.at[s], dst_ref=recv.at[s], send_sem=zsend.at[s], recv_sem=zrecv.at[s],
                    device_id={"shard": s}, device_id_type=MESH,
                ).wait_recv()

            @pl.when(s == me)
            def _():
                zlocal().wait()

            docs = recv[s].astype(F32)
            for i in range(PADDED):
                stage[pl.ds(i * 64 + e, 8, stride=8), :] = docs[8 * i : 8 * i + 8, :]

        @pl.loop(0, GROUP // 16)
        def _(a):
            v = stage[pl.ds(pl.multiple_of(a * 128, 8), 128), :]
            part = []
            for h in range(2):
                tiles = [v[64 * h + 8 * j : 64 * h + 8 * j + 8, :] for j in range(8)]
                square = tiles[0] * tiles[0]
                for j in range(1, 8):
                    square = square + tiles[j] * tiles[j]
                scale = lax.rsqrt(jnp.sum(square, axis=1, keepdims=True) + 1e-06)
                part.append([tile * scale for tile in tiles])
            for j in range(8):
                q[0, g, pl.ds(pl.multiple_of(a * 16, 16), 16), 128 * j : 128 * j + 128] = jnp.concatenate(
                    [part[0][j], part[1][j]], axis=0
                ).astype(BF16)

        ycopy(n, 0).start()

        @pl.when(role == 3)
        def _():
            ycopy(n, 1).start()

    away = lax.broadcasted_iota(jnp.int32, (GROUP, 256), 0) - lax.broadcasted_iota(jnp.int32, (GROUP, 256), 1)

    def tile(pa, ga, pb, gb, diagonal):
        g = lax.dot_general(q[pa, ga, 0:GROUP, :], q[pb, gb], LAST, preferred_element_type=F32)
        yb = jnp.where(pb == 0, y0, jnp.where(pb == 1, y1, y2))
        left = cs[pl.ds(pl.multiple_of((pa * NG + ga) * 256, 8), GROUP), :]
        right = cl[yb * NG + gb]
        at = pl.multiple_of((pa * NG + ga) * GROUP, 8)
        rows = ra[pl.ds(at, GROUP), :]
        for h in range(2):
            same = left.reshape(PADDED, 8, 128) == right[None, :, 128 * h : 128 * h + 128]
            if diagonal is not None:
                away_h = away[:, 128 * h : 128 * h + 128].reshape(PADDED, 8, 128)
                same = same & (away_h != jnp.where(diagonal, 0, 4096))
            vals = jnp.where(same, g[:, 128 * h : 128 * h + 128].reshape(PADDED, 8, 128), -1.0)
            rows = jnp.maximum(rows, vals.reshape(GROUP, 128))
            at_c = pb * NG + gb
            colacc[at_c, :, 128 * h : 128 * h + 128] = jnp.maximum(
                colacc[at_c, :, 128 * h : 128 * h + 128], jnp.max(vals, axis=0)
            )
        ra[pl.ds(at, GROUP), :] = rows

    def before(n):
        g = group_of(n)

        @pl.when(role != 3)
        def _():
            @pl.loop(0, n)
            def _(m):
                gm = group_of(m)
                tile(0, g, jnp.where(role == 2, 2, 1), gm, None)
                tile(0, g, jnp.where(role == 1, 2, 0), gm, None)

        @pl.when(role == 3)
        def _():
            @pl.loop(0, n)
            def _(m):
                tile(0, g, 0, group_of(m), None)

        @pl.when(role != 1)
        def _():
            tile(0, g, 0, g, True)

    def after(n):
        g = group_of(n)

        @pl.when(role != 3)
        def _():
            ywait(n, 0)

        @pl.when(role == 0)
        def _():
            @pl.loop(0, n + 1)
            def _(m):
                tile(0, group_of(m), 1, g, None)

        @pl.when((role == 1) | (role == 2))
        def _():
            ywait(n, 1)

            @pl.loop(0, n)
            def _(m):
                gm = group_of(m)
                tile(0, gm, 2, g, None)
                tile(1, g, 2, gm, None)
                tile(1, gm, 2, g, None)
                tile(jnp.where(role == 1, 0, 1), gm, 1, g, None)

            tile(0, g, 2, g, None)
            tile(1, g, 2, g, None)
            tile(jnp.where(role == 1, 0, 1), g, 1, g, role == 2)

    @pl.loop(0, NG + 1)
    def _(n):
        @pl.when(n < NG)
        def _():
            arrive(n)

        @pl.when(n > 0)
        def _():
            after(n - 1)

        @pl.when(n < NG)
        def _():
            before(n)

    spot8 = lax.broadcasted_iota(jnp.int32, (8, 256), 1) % 8 == lax.broadcasted_iota(jnp.int32, (8, 256), 0)
    out_lane = lax.broadcasted_iota(jnp.int32, (256, 128), 1) % PART
    gather = (lax.broadcasted_iota(jnp.int32, (256, 128), 0) // 8 == out_lane).astype(F32).astype(BF16)
    lane8 = lax.broadcasted_iota(jnp.int32, (8, 128), 1)
    tsrc[...] = jnp.full(tsrc.shape, -1.0, F32)

    @pl.loop(0, 3)
    def _(p):
        yp = jnp.where(p == 0, y0, jnp.where(p == 1, y1, y2))
        parts = ([], [], [])
        for g in range(NG):
            col = jnp.max(colacc[p * NG + g], axis=0, keepdims=True)
            for part, kept in zip(parts, pieces(col)):
                part.append(jnp.where(spot8, kept, 0.0).astype(BF16).astype(F32))
        best = 0.0
        for part in parts:
            left = jnp.concatenate(part, axis=0).astype(BF16)
            best = best + jnp.dot(left, gather, preferred_element_type=F32)
        mine = lax.broadcasted_iota(jnp.int32, (NS, 128), 1) // PART == yp
        tsrc[...] = jnp.maximum(tsrc[...], jnp.where(mine, best, -1.0))

    @pl.loop(0, 2 * NG)
    def _(k):
        yp = jnp.where(k // NG == 0, y0, y1)
        rows = ra[pl.ds(pl.multiple_of(k * GROUP, 8), GROUP), :].reshape(PADDED, 8, 128)
        rows = jnp.max(rows, axis=2, keepdims=True)
        best = jnp.full((8, 128), -1.0, F32)
        for i in range(PART):
            best = jnp.where(lane8 % PART == i, rows[i], best)
        at = pl.ds(pl.multiple_of((k % NG) * 8, 8), 8)
        tsrc[at, :] = jnp.maximum(tsrc[at, :], jnp.where(lane8 // PART == yp, best, -1.0))

    def r1(k):
        dev = (rep + k) % NR
        return pltpu.make_async_remote_copy(
            src_ref=tsrc.at[pl.ds(pl.multiple_of(dev * 16, 16), 16)], dst_ref=trecv.at[k],
            send_sem=r1send.at[k], recv_sem=r1recv.at[k], device_id={"rep": dev}, device_id_type=MESH,
        )

    for k in range(1, NR):
        r1(k).start()

    @pl.loop(1, NS)
    def _(k):
        zcopy((me + k) % NS).wait_send()

    @pl.loop(0, NG)
    def _(n):
        ycopy(n, 0).wait_send()

        @pl.when(role == 3)
        def _():
            ycopy(n, 1).wait_send()

    for k in range(1, NR):
        r1(k).wait_recv()
    full = tsrc[pl.ds(pl.multiple_of(rep * 16, 16), 16), :]
    full = jnp.maximum(jnp.maximum(full, trecv[1]), jnp.maximum(trecv[2], trecv[3]))
    for r in range(16):
        trow[r] = full[r : r + 1, :]

    def source(r):
        e, g = r % 8, 2 * rep + r // 8
        return ((e // 2) * 2 + g % 2) * 8 + (g // 2) * 2 + e % 2

    def r2(r):
        return pltpu.make_async_remote_copy(
            src_ref=trow.at[r], dst_ref=vrecv.at[me], send_sem=r2send.at[r], recv_sem=r2recv.at[me],
            device_id={"shard": source(r)}, device_id_type=MESH,
        )

    @pl.loop(0, 16)
    def _(r):
        @pl.when(source(r) != me)
        def _():
            r2(r).start()

        @pl.when(source(r) == me)
        def _():
            vrecv[me] = trow[r]

    def r3(k):
        return pltpu.make_async_remote_copy(
            src_ref=res, dst_ref=res, send_sem=r3send.at[k], recv_sem=r3recv,
            device_id={"rep": (rep + k) % NR}, device_id_type=MESH,
        )

    @pl.when(x == rep)
    def _():
        @pl.loop(1, NS)
        def _(k):
            s = (me + k) % NS
            pltpu.make_async_remote_copy(
                src_ref=trow.at[0], dst_ref=vrecv.at[s], send_sem=r2send.at[0], recv_sem=r2recv.at[s],
                device_id={"shard": s}, device_id_type=MESH,
            ).wait_recv()

        sub64 = lax.broadcasted_iota(jnp.int32, (64, 128), 0)
        high = ctmp[...]
        high = jnp.where(high >= 0, high // 128, -1)
        for o in range(NS):
            hit = sub64 == high[o : o + 1, :]
            for w, kept in enumerate(pieces(vrecv[o])):
                emb[o // 8, 64 * w : 64 * w + 64, 128 * (o % 8) : 128 * (o % 8) + 128] = jnp.where(
                    hit, kept, 0.0
                ).astype(BF16)
        done = 0.0
        for j in range(8):
            done = done + lax.dot_general(
                emb[j, 0:192, :], emb[j, 192:320, :], LAST, preferred_element_type=F32
            )
        res[...] = (done[0:64, :] + done[64:128, :] + done[128:192, :])[0:56, :]
        for k in range(1, NR):
            r3(k).start()
        for k in range(1, NR):
            r3(k).wait_send()

    @pl.when(x != rep)
    def _():
        r3(1).wait_recv()

    out_ref[...] = res[0:FLAT, :]

    @pl.loop(0, 16)
    def _(r):
        @pl.when(source(r) != me)
        def _():
            r2(r).wait_send()

    for k in range(1, NR):
        r1(k).wait_send()


def shards(embeddings, send_index, place_index, slot_cluster, pair_list):
    vm = pl.BlockSpec(memory_space=pltpu.VMEM)
    hbm = pl.BlockSpec(memory_space=pl.ANY)
    dma = pltpu.SemaphoreType.DMA
    out = pl.pallas_call(
        kernel,
        out_shape=jax.ShapeDtypeStruct((DOCS // 128, 128), F32),
        in_specs=[hbm] * 5,
        out_specs=vm,
        scratch_shapes=[
            pltpu.SMEM((DOCS,), jnp.int32),
            pltpu.SMEM(slot_cluster.shape, jnp.int32),
            pltpu.VMEM((FLAT, 128), jnp.int32),
            pltpu.VMEM((FLAT, 128), jnp.int32),
            pltpu.VMEM((DOCS * 8, 128), F32),
            pltpu.VMEM((3, NG, 256, D), BF16),
            pltpu.VMEM((NS, MSG, 128), BF16),
            pltpu.VMEM((NS, MSG, 128), BF16),
            pltpu.VMEM((NBUF, CHUNK, D), BF16),
            pltpu.VMEM((GROUP * 8, 128), F32),
            pltpu.VMEM((2 * NG * 256, 128), F32),
            pltpu.VMEM((2 * NG * GROUP, 128), F32),
            pltpu.VMEM((3 * NG, 8, 256), F32),
            pltpu.VMEM((NR * NG, 8, 256), F32),
            pltpu.VMEM((NS, 128), jnp.int32),
            pltpu.VMEM((NS, 128), F32),
            pltpu.VMEM((NR, 16, 128), F32),
            pltpu.VMEM((16, 1, 128), F32),
            pltpu.VMEM((NS, 1, 128), F32),
            pltpu.VMEM((56, 128), F32),
            dma((4,)),
            pltpu.SemaphoreType.REGULAR,
            dma((NBUF,)),
            dma((NS,)),
            dma((NS,)),
            dma((2, NG)),
            dma((2, NG)),
            dma((NR,)),
            dma((NR,)),
            dma((16,)),
            dma((NS,)),
            dma((NR,)),
            dma(()),
        ],
        compiler_params=pltpu.CompilerParams(
            collective_id=0, has_side_effects=True, vmem_limit_bytes=62 * 1024 * 1024
        ),
        name="dedup",
    )(
        send_index, slot_cluster, embeddings, send_index.reshape(FLAT, 128), place_index.reshape(FLAT, 128)
    )
    return out.reshape(-1)


def solution(mesh):
    return jax.shard_map(
        shards,
        mesh=mesh,
        in_specs=(P("shard", None), P("shard"), P("shard"), P("shard"), P(("shard", "rep"), None)),
        out_specs=P("shard"),
        check_vma=False,
    )
```

```python
import functools

import jax
import jax.numpy as jnp
from jax import lax
from jax.experimental import pallas as pl
from jax.experimental.pallas import tpu as pltpu
from jax.sharding import PartitionSpec as P

D = 1024
BLK = 256
DOCS = 6400
NS = 64
NR = 4
SHARE = 100
PART = 25
PADDED = 26
MSG = PADDED * 8
GROUP = PADDED * 8
NG = 8
CHUNK = 400
NCHUNK = DOCS // CHUNK
NBUF = 8
FLAT = DOCS // 128
MESH = pl.DeviceIdType.MESH
F32 = jnp.float32
BF16 = jnp.bfloat16
LAST = (((1,), (1,)), ((), ()))


def pieces(v):
    a = v.astype(BF16).astype(F32)
    r = v - a
    b = r.astype(BF16).astype(F32)
    return a, b, r - b


def kernel(
    send_hbm, table_hbm, emb_ref, idx_hbm, place_hbm, out_ref,
    send_ref, table_ref, idx_ref, place_ref,
    wide, q, outb, recv, emb, stage, cs, ra, colacc, cl, ctmp, tsrc, trecv, trow, vrecv, res,
    isem, bsem, esem, zsend, zrecv, ysend, yrecv, r1send, r1recv, r2send, r2recv, r3send, r3recv,
):
    me = lax.axis_index("shard")
    rep = lax.axis_index("rep")
    z, x, c = me // 8, (me // 2) % 4, me % 2
    def rep_of(r):
        return (r + 2 * c) % 4

    def pick(a, b, c_, d):
        return jnp.where(role == 0, a, jnp.where(role == 1, b, jnp.where(role == 2, c_, d)))

    role = rep_of(rep)
    y0 = rep
    y1 = rep_of(pick(3, 0, 1, 3))
    y2 = rep_of(pick(0, 2, 3, 0))

    def fetch(ch, slot):
        return pltpu.make_async_copy(
            emb_ref.at[pl.ds(pl.multiple_of(ch * CHUNK, 16), CHUNK)], emb.at[slot], esem.at[slot]
        )

    ints = [
        pltpu.make_async_copy(a, b, isem.at[i])
        for i, (a, b) in enumerate(
            [(send_hbm, send_ref), (table_hbm, table_ref), (idx_hbm, idx_ref), (place_hbm, place_ref)]
        )
    ]
    def in_line(k):
        other = (z * 2 + c + k) % 16
        return {"shard": (other // 2) * 8 + x * 2 + other % 2}

    def in_ring(k):
        return {"shard": z * 8 + ((x + k) % 4) * 2 + c}

    barrier = pltpu.get_barrier_semaphore()
    for k in range(1, NR):
        pl.semaphore_signal(barrier, inc=1, device_id={"rep": (rep + k) % NR}, device_id_type=MESH)
    for k in range(1, 4):
        pl.semaphore_signal(barrier, inc=1, device_id=in_ring(k), device_id_type=MESH)
    for k in range(1, 16):
        pl.semaphore_signal(barrier, inc=1, device_id=in_line(k), device_id_type=MESH)

    for i in range(NBUF):
        fetch(i, i).start()
    for copy in ints:
        copy.start()

    @pl.loop(0, NCHUNK)
    def _(ch):
        slot = ch % NBUF
        fetch(ch, slot).wait()

        @pl.loop(0, CHUNK // 16, unroll=5)
        def _(r):
            rows = emb[slot, pl.ds(pl.multiple_of(r * 16, 16), 16), :].astype(F32)
            base = ch * (CHUNK * 8) + r * 128
            for h in range(2):
                for j in range(8):
                    wide[pl.ds(pl.multiple_of(base + h * 64 + j * 8, 8), 8), :] = rows[
                        8 * h : 8 * h + 8, 128 * j : 128 * j + 128
                    ]

        @pl.when(ch + NBUF < NCHUNK)
        def _():
            fetch(ch + NBUF, slot).start()

    for copy in ints:
        copy.wait()
    pl.semaphore_wait(barrier, 15 + 3 + NR - 1)
    for k in range(1, 4):
        pl.semaphore_signal(bsem, inc=1, device_id=in_ring(k), device_id_type=MESH)

    def zcopy(dst):
        return pltpu.make_async_remote_copy(
            src_ref=outb.at[dst], dst_ref=recv.at[me], send_sem=zsend.at[dst], recv_sem=zrecv.at[me],
            device_id={"shard": dst}, device_id_type=MESH,
        )

    def zlocal():
        return pltpu.make_async_copy(outb.at[me], recv.at[me], zrecv.at[me])

    def address(i):
        return (i // 8) * 64 + i % 8

    def send(k):
        n = k // 8
        t, h, w, b = n // 2, n % 2, (k // 2) % 4, k % 2
        dst = ((z + h + 2 * w) % 8) * 8 + ((x + t) % 4) * 2 + (c + b) % 2
        base = dst * SHARE + rep * PART
        for a in range(PADDED // 2):
            i0 = send_ref[base + 2 * a]
            i1 = send_ref[base + min(2 * a + 1, PART - 1)]
            v0 = wide[pl.ds(address(i0), 8, stride=8), :]
            v1 = wide[pl.ds(address(i1), 8, stride=8), :]
            outb[dst, pl.ds(16 * a, 16), :] = jnp.concatenate([v0, v1], axis=0).astype(BF16)

        @pl.when(dst != me)
        def _():
            zcopy(dst).start()

        @pl.when(dst == me)
        def _():
            zlocal().start()

    @pl.loop(0, 16)
    def _(k):
        send(k)

    pl.semaphore_wait(bsem, 3)

    @pl.loop(16, NS)
    def _(k):
        send(k)

    lane1 = lax.broadcasted_iota(jnp.int32, (1, 128), 1)

    def share_of(flat, o):
        a, off = o * SHARE // 128, o * SHARE % 128
        b = min(a + 1, FLAT - 1)
        both = jnp.where(lane1 >= off, flat[a : a + 1, :], flat[b : b + 1, :])
        both = both if off == 0 else pltpu.roll(both, 128 - off, 1)
        return jnp.where(lane1 < SHARE, both, -1)

    for g in range(NG):
        for e in range(8):
            s = ((e // 2) * 2 + g % 2) * 8 + (g // 2) * 2 + e % 2
            ctmp[8 * g + e : 8 * g + e + 1, :] = share_of(place_ref, s)
    block = ctmp[...] // BLK
    ids = jnp.full((NS, 128), -1.0, F32)
    for b in range(table_ref.shape[0] // BLK):
        ids = jnp.where(block == b, (table_ref[b * BLK] - me * 26).astype(F32), ids)
    ordered = ids.astype(BF16)
    lane = lax.broadcasted_iota(jnp.int32, (128, 256), 0)
    spot = lax.broadcasted_iota(jnp.int32, (128, 256), 1)
    keep = (lax.broadcasted_iota(jnp.int32, (NS, 256), 1) % 8) == (
        lax.broadcasted_iota(jnp.int32, (NS, 256), 0) % 8
    )
    for y in range(NR):
        spread = ((lane == PART * y + spot // 8) & (spot < 8 * PART)).astype(F32).astype(BF16)
        ids_y = jnp.dot(ordered, spread, preferred_element_type=F32)
        ids_y = jnp.where(keep, ids_y, 0.0)
        for g in range(NG):
            row = jnp.sum(ids_y[8 * g : 8 * g + 8, :], axis=0, keepdims=True)
            cl[y * NG + g] = jnp.broadcast_to(jnp.where(spot[0:1, :] < 8 * PART, row, -1.0), (8, 256))

    @pl.loop(0, 2 * NG)
    def _(k):
        y = jnp.where(k // NG == 0, y0, y1)
        rows = cl[y * NG + k % NG]
        for h in range(2):
            tile = jnp.broadcast_to(rows[0:1, 128 * h : 128 * h + 128], (128, 128))
            cs[pl.ds(pl.multiple_of(k * 256 + h * 128, 8), 128), :] = tile.T

    ra[...] = jnp.full(ra.shape, -1.0, F32)
    colacc[...] = jnp.full(colacc.shape, -1.0, F32)

    @pl.loop(0, 3 * NG)
    def _(k):
        q[k // NG, k % NG, GROUP:256, :] = jnp.zeros((256 - GROUP, D), BF16)

    sub = lax.broadcasted_iota(jnp.int32, (128, 128), 0)
    for o in range(NS):
        low = share_of(idx_ref, o)
        ctmp[o : o + 1, :] = low
        low = jnp.where(low >= 0, low % 128, -1)
        emb[o // 8, 192:320, 128 * (o % 8) : 128 * (o % 8) + 128] = (sub == low).astype(F32).astype(BF16)

    def group_of(n):
        return ((x - n // 2 + 4) % 4) * 2 + (z + n) % 2

    def ycopy(n, which):
        g = group_of(n)
        at = jnp.where(role >= 2, 1, 0) if which == 0 else 0
        dev = rep_of(pick(1, 2, 1, 2)) if which == 0 else rep_of(0)
        return pltpu.make_async_remote_copy(
            src_ref=q.at[0, g, pl.ds(0, GROUP)], dst_ref=q.at[1 + at, g, pl.ds(0, GROUP)],
            send_sem=ysend.at[which, n], recv_sem=yrecv.at[at, n],
            device_id={"rep": dev}, device_id_type=MESH,
        )

    def ywait(n, at):
        g = group_of(n)
        pltpu.make_async_remote_copy(
            src_ref=q.at[0, g, pl.ds(0, GROUP)], dst_ref=q.at[1 + at, g, pl.ds(0, GROUP)],
            send_sem=ysend.at[0, n], recv_sem=yrecv.at[at, n],
            device_id={"rep": rep_of(pick(1, 2, 1, 2))}, device_id_type=MESH,
        ).wait_recv()

    def arrive(n):
        g = group_of(n)
        xs, zs = g // 2, g % 2

        @pl.loop(0, 8)
        def _(e):
            s = ((e // 2) * 2 + zs) * 8 + xs * 2 + e % 2

            @pl.when(s != me)
            def _():
                pltpu.make_async_remote_copy(
                    src_ref=outb.at[s], dst_ref=recv.at[s], send_sem=zsend.at[s], recv_sem=zrecv.at[s],
                    device_id={"shard": s}, device_id_type=MESH,
                ).wait_recv()

            @pl.when(s == me)
            def _():
                zlocal().wait()

            docs = recv[s].astype(F32)
            for i in range(PADDED):
                stage[pl.ds(i * 64 + e, 8, stride=8), :] = docs[8 * i : 8 * i + 8, :]

        @pl.loop(0, GROUP // 16)
        def _(a):
            v = stage[pl.ds(pl.multiple_of(a * 128, 8), 128), :]
            part = []
            for h in range(2):
                tiles = [v[64 * h + 8 * j : 64 * h + 8 * j + 8, :] for j in range(8)]
                square = tiles[0] * tiles[0]
                for j in range(1, 8):
                    square = square + tiles[j] * tiles[j]
                scale = lax.rsqrt(jnp.sum(square, axis=1, keepdims=True) + 1e-06)
                part.append([tile * scale for tile in tiles])
            for j in range(8):
                q[0, g, pl.ds(pl.multiple_of(a * 16, 16), 16), 128 * j : 128 * j + 128] = jnp.concatenate(
                    [part[0][j], part[1][j]], axis=0
                ).astype(BF16)

        @pl.when(role == 3)
        def _():
            ycopy(n, 1).start()

        ycopy(n, 0).start()

    away = lax.broadcasted_iota(jnp.int32, (GROUP, 256), 0) - lax.broadcasted_iota(jnp.int32, (GROUP, 256), 1)

    def tile(pa, ga, pb, gb, diagonal):
        g = lax.dot_general(q[pa, ga, 0:GROUP, :], q[pb, gb], LAST, preferred_element_type=F32)
        yb = jnp.where(pb == 0, y0, jnp.where(pb == 1, y1, y2))
        left = cs[pl.ds(pl.multiple_of((pa * NG + ga) * 256, 8), GROUP), :]
        right = cl[yb * NG + gb]
        at = pl.multiple_of((pa * NG + ga) * GROUP, 8)
        rows = ra[pl.ds(at, GROUP), :]
        for h in range(2):
            same = left.reshape(PADDED, 8, 128) == right[None, :, 128 * h : 128 * h + 128]
            if diagonal is not None:
                away_h = away[:, 128 * h : 128 * h + 128].reshape(PADDED, 8, 128)
                same = same & (away_h != jnp.where(diagonal, 0, 4096))
            vals = jnp.where(same, g[:, 128 * h : 128 * h + 128].reshape(PADDED, 8, 128), -1.0)
            rows = jnp.maximum(rows, vals.reshape(GROUP, 128))
            at_c = pb * NG + gb
            colacc[at_c, :, 128 * h : 128 * h + 128] = jnp.maximum(
                colacc[at_c, :, 128 * h : 128 * h + 128], jnp.max(vals, axis=0)
            )
        ra[pl.ds(at, GROUP), :] = rows

    def before(n):
        g = group_of(n)

        @pl.when(role != 3)
        def _():
            @pl.loop(0, n)
            def _(m):
                gm = group_of(m)
                tile(0, g, jnp.where(role == 2, 2, 1), gm, None)
                tile(0, g, jnp.where(role == 1, 2, 0), gm, None)

        @pl.when(role == 3)
        def _():
            @pl.loop(0, n)
            def _(m):
                tile(0, g, 0, group_of(m), None)

        @pl.when(role != 1)
        def _():
            tile(0, g, 0, g, True)

    def after(n):
        g = group_of(n)

        @pl.when(role != 3)
        def _():
            ywait(n, 0)

        @pl.when(role == 0)
        def _():
            @pl.loop(0, n + 1)
            def _(m):
                tile(0, group_of(m), 1, g, None)

        @pl.when((role == 1) | (role == 2))
        def _():
            ywait(n, 1)

            @pl.loop(0, n)
            def _(m):
                gm = group_of(m)
                tile(0, gm, 2, g, None)
                tile(1, g, 2, gm, None)
                tile(1, gm, 2, g, None)
                tile(jnp.where(role == 1, 0, 1), gm, 1, g, None)

            tile(0, g, 2, g, None)
            tile(1, g, 2, g, None)
            tile(jnp.where(role == 1, 0, 1), g, 1, g, role == 2)

    @pl.loop(0, NG + 1)
    def _(n):
        @pl.when(n < NG)
        def _():
            arrive(n)

        @pl.when(n > 0)
        def _():
            after(n - 1)

        @pl.when(n < NG)
        def _():
            before(n)

    spot8 = lax.broadcasted_iota(jnp.int32, (8, 256), 1) % 8 == lax.broadcasted_iota(jnp.int32, (8, 256), 0)
    out_lane = lax.broadcasted_iota(jnp.int32, (256, 128), 1) % PART
    gather = (lax.broadcasted_iota(jnp.int32, (256, 128), 0) // 8 == out_lane).astype(F32).astype(BF16)
    lane8 = lax.broadcasted_iota(jnp.int32, (8, 128), 1)
    tsrc[...] = jnp.full(tsrc.shape, -1.0, F32)

    @pl.loop(0, 3)
    def _(p):
        yp = jnp.where(p == 0, y0, jnp.where(p == 1, y1, y2))
        parts = ([], [], [])
        for g in range(NG):
            col = jnp.max(colacc[p * NG + g], axis=0, keepdims=True)
            for part, kept in zip(parts, pieces(col)):
                part.append(jnp.where(spot8, kept, 0.0).astype(BF16).astype(F32))
        best = 0.0
        for part in parts:
            left = jnp.concatenate(part, axis=0).astype(BF16)
            best = best + jnp.dot(left, gather, preferred_element_type=F32)
        mine = lax.broadcasted_iota(jnp.int32, (NS, 128), 1) // PART == yp
        tsrc[...] = jnp.maximum(tsrc[...], jnp.where(mine, best, -1.0))

    @pl.loop(0, 2 * NG)
    def _(k):
        yp = jnp.where(k // NG == 0, y0, y1)
        rows = ra[pl.ds(pl.multiple_of(k * GROUP, 8), GROUP), :].reshape(PADDED, 8, 128)
        rows = jnp.max(rows, axis=2, keepdims=True)
        best = jnp.full((8, 128), -1.0, F32)
        for i in range(PART):
            best = jnp.where(lane8 % PART == i, rows[i], best)
        at = pl.ds(pl.multiple_of((k % NG) * 8, 8), 8)
        tsrc[at, :] = jnp.maximum(tsrc[at, :], jnp.where(lane8 // PART == yp, best, -1.0))

    def r1(k):
        dev = (rep + k) % NR
        return pltpu.make_async_remote_copy(
            src_ref=tsrc.at[pl.ds(pl.multiple_of(dev * 16, 16), 16)], dst_ref=trecv.at[k],
            send_sem=r1send.at[k], recv_sem=r1recv.at[k], device_id={"rep": dev}, device_id_type=MESH,
        )

    for k in range(1, NR):
        r1(k).start()

    @pl.loop(1, NS)
    def _(k):
        zcopy((me + k) % NS).wait_send()

    @pl.loop(0, NG)
    def _(n):
        ycopy(n, 0).wait_send()

        @pl.when(role == 3)
        def _():
            ycopy(n, 1).wait_send()

    for k in range(1, NR):
        r1(k).wait_recv()
    full = tsrc[pl.ds(pl.multiple_of(rep * 16, 16), 16), :]
    full = jnp.maximum(jnp.maximum(full, trecv[1]), jnp.maximum(trecv[2], trecv[3]))
    for r in range(16):
        trow[r] = full[r : r + 1, :]

    def source(r):
        e, g = r % 8, 2 * rep + r // 8
        return ((e // 2) * 2 + g % 2) * 8 + (g // 2) * 2 + e % 2

    def r2(r):
        return pltpu.make_async_remote_copy(
            src_ref=trow.at[r], dst_ref=vrecv.at[me], send_sem=r2send.at[r], recv_sem=r2recv.at[me],
            device_id={"shard": source(r)}, device_id_type=MESH,
        )

    @pl.loop(0, 16)
    def _(r):
        @pl.when(source(r) != me)
        def _():
            r2(r).start()

        @pl.when(source(r) == me)
        def _():
            vrecv[me] = trow[r]

    def r3(k):
        return pltpu.make_async_remote_copy(
            src_ref=res, dst_ref=res, send_sem=r3send.at[k], recv_sem=r3recv,
            device_id={"rep": (rep + k) % NR}, device_id_type=MESH,
        )

    @pl.when(x == rep)
    def _():
        @pl.loop(1, NS)
        def _(k):
            s = (me + k) % NS
            pltpu.make_async_remote_copy(
                src_ref=trow.at[0], dst_ref=vrecv.at[s], send_sem=r2send.at[0], recv_sem=r2recv.at[s],
                device_id={"shard": s}, device_id_type=MESH,
            ).wait_recv()

        sub64 = lax.broadcasted_iota(jnp.int32, (64, 128), 0)
        high = ctmp[...]
        high = jnp.where(high >= 0, high // 128, -1)
        for o in range(NS):
            hit = sub64 == high[o : o + 1, :]
            for w, kept in enumerate(pieces(vrecv[o])):
                emb[o // 8, 64 * w : 64 * w + 64, 128 * (o % 8) : 128 * (o % 8) + 128] = jnp.where(
                    hit, kept, 0.0
                ).astype(BF16)
        done = 0.0
        for j in range(8):
            done = done + lax.dot_general(
                emb[j, 0:192, :], emb[j, 192:320, :], LAST, preferred_element_type=F32
            )
        res[...] = (done[0:64, :] + done[64:128, :] + done[128:192, :])[0:56, :]
        for k in range(1, NR):
            r3(k).start()
        for k in range(1, NR):
            r3(k).wait_send()

    @pl.when(x != rep)
    def _():
        r3(1).wait_recv()

    out_ref[...] = res[0:FLAT, :]

    @pl.loop(0, 16)
    def _(r):
        @pl.when(source(r) != me)
        def _():
            r2(r).wait_send()

    for k in range(1, NR):
        r1(k).wait_send()


def shards(embeddings, send_index, place_index, slot_cluster, pair_list):
    vm = pl.BlockSpec(memory_space=pltpu.VMEM)
    hbm = pl.BlockSpec(memory_space=pl.ANY)
    dma = pltpu.SemaphoreType.DMA
    out = pl.pallas_call(
        kernel,
        out_shape=jax.ShapeDtypeStruct((DOCS // 128, 128), F32),
        in_specs=[hbm] * 5,
        out_specs=vm,
        scratch_shapes=[
            pltpu.SMEM((DOCS,), jnp.int32),
            pltpu.SMEM(slot_cluster.shape, jnp.int32),
            pltpu.VMEM((FLAT, 128), jnp.int32),
            pltpu.VMEM((FLAT, 128), jnp.int32),
            pltpu.VMEM((DOCS * 8, 128), F32),
            pltpu.VMEM((3, NG, 256, D), BF16),
            pltpu.VMEM((NS, MSG, 128), BF16),
            pltpu.VMEM((NS, MSG, 128), BF16),
            pltpu.VMEM((NBUF, CHUNK, D), BF16),
            pltpu.VMEM((GROUP * 8, 128), F32),
            pltpu.VMEM((2 * NG * 256, 128), F32),
            pltpu.VMEM((2 * NG * GROUP, 128), F32),
            pltpu.VMEM((3 * NG, 8, 256), F32),
            pltpu.VMEM((NR * NG, 8, 256), F32),
            pltpu.VMEM((NS, 128), jnp.int32),
            pltpu.VMEM((NS, 128), F32),
            pltpu.VMEM((NR, 16, 128), F32),
            pltpu.VMEM((16, 1, 128), F32),
            pltpu.VMEM((NS, 1, 128), F32),
            pltpu.VMEM((56, 128), F32),
            dma((4,)),
            pltpu.SemaphoreType.REGULAR,
            dma((NBUF,)),
            dma((NS,)),
            dma((NS,)),
            dma((2, NG)),
            dma((2, NG)),
            dma((NR,)),
            dma((NR,)),
            dma((16,)),
            dma((NS,)),
            dma((NR,)),
            dma(()),
        ],
        compiler_params=pltpu.CompilerParams(
            collective_id=0, has_side_effects=True, vmem_limit_bytes=62 * 1024 * 1024
        ),
        name="dedup",
    )(
        send_index, slot_cluster, embeddings, send_index.reshape(FLAT, 128), place_index.reshape(FLAT, 128)
    )
    return out.reshape(-1)


def solution(mesh):
    return jax.shard_map(
        shards,
        mesh=mesh,
        in_specs=(P("shard", None), P("shard"), P("shard"), P("shard"), P(("shard", "rep"), None)),
        out_specs=P("shard"),
        check_vma=False,
    )
```

```python
import functools

import jax
import jax.numpy as jnp
from jax import lax
from jax.experimental import pallas as pl
from jax.experimental.pallas import tpu as pltpu
from jax.sharding import PartitionSpec as P

D = 1024
BLK = 256
DOCS = 6400
NS = 64
NR = 4
SHARE = 100
PART = 25
PADDED = 26
MSG = PADDED * 8
GROUP = PADDED * 8
NG = 8
CHUNK = 400
NCHUNK = DOCS // CHUNK
NBUF = 8
FLAT = DOCS // 128
MESH = pl.DeviceIdType.MESH
F32 = jnp.float32
BF16 = jnp.bfloat16
LAST = (((1,), (1,)), ((), ()))


def pieces(v):
    a = v.astype(BF16).astype(F32)
    r = v - a
    b = r.astype(BF16).astype(F32)
    return a, b, r - b


def kernel(
    send_hbm, table_hbm, emb_ref, idx_hbm, place_hbm, out_ref,
    send_ref, table_ref, idx_ref, place_ref,
    wide, q, outb, recv, emb, stage, cs, ra, colacc, cl, ctmp, tsrc, trecv, trow, vrecv, res,
    isem, bsem, esem, zsend, zrecv, ysend, yrecv, r1send, r1recv, r2send, r2recv, r3send, r3recv,
):
    me = lax.axis_index("shard")
    rep = lax.axis_index("rep")
    z, x, c = me // 8, (me // 2) % 4, me % 2
    def rep_of(r):
        return jnp.where(c == 0, r, (4 - r) % 4)

    def pick(a, b, c_, d):
        return jnp.where(role == 0, a, jnp.where(role == 1, b, jnp.where(role == 2, c_, d)))

    role = rep_of(rep)
    y0 = rep
    y1 = rep_of(pick(1, 1, 1, 0))
    y2 = rep_of(pick(3, 1, 3, 2))

    def fetch(ch, slot):
        return pltpu.make_async_copy(
            emb_ref.at[pl.ds(pl.multiple_of(ch * CHUNK, 16), CHUNK)], emb.at[slot], esem.at[slot]
        )

    ints = [
        pltpu.make_async_copy(a, b, isem.at[i])
        for i, (a, b) in enumerate(
            [(send_hbm, send_ref), (table_hbm, table_ref), (idx_hbm, idx_ref), (place_hbm, place_ref)]
        )
    ]
    def in_line(k):
        other = (z * 2 + c + k) % 16
        return {"shard": (other // 2) * 8 + x * 2 + other % 2}

    def in_ring(k):
        return {"shard": z * 8 + ((x + k) % 4) * 2 + c}

    barrier = pltpu.get_barrier_semaphore()
    for k in range(1, NR):
        pl.semaphore_signal(barrier, inc=1, device_id={"rep": (rep + k) % NR}, device_id_type=MESH)
    for k in range(1, 4):
        pl.semaphore_signal(barrier, inc=1, device_id=in_ring(k), device_id_type=MESH)
    for k in range(1, 16):
        pl.semaphore_signal(barrier, inc=1, device_id=in_line(k), device_id_type=MESH)

    for i in range(NBUF):
        fetch(i, i).start()
    for copy in ints:
        copy.start()

    @pl.loop(0, NCHUNK)
    def _(ch):
        slot = ch % NBUF
        fetch(ch, slot).wait()

        @pl.loop(0, CHUNK // 16, unroll=5)
        def _(r):
            rows = emb[slot, pl.ds(pl.multiple_of(r * 16, 16), 16), :].astype(F32)
            base = ch * (CHUNK * 8) + r * 128
            for h in range(2):
                for j in range(8):
                    wide[pl.ds(pl.multiple_of(base + h * 64 + j * 8, 8), 8), :] = rows[
                        8 * h : 8 * h + 8, 128 * j : 128 * j + 128
                    ]

        @pl.when(ch + NBUF < NCHUNK)
        def _():
            fetch(ch + NBUF, slot).start()

    for copy in ints:
        copy.wait()
    pl.semaphore_wait(barrier, 15 + 3 + NR - 1)
    for k in range(1, 4):
        pl.semaphore_signal(bsem, inc=1, device_id=in_ring(k), device_id_type=MESH)

    def zcopy(dst):
        return pltpu.make_async_remote_copy(
            src_ref=outb.at[dst], dst_ref=recv.at[me], send_sem=zsend.at[dst], recv_sem=zrecv.at[me],
            device_id={"shard": dst}, device_id_type=MESH,
        )

    def zlocal():
        return pltpu.make_async_copy(outb.at[me], recv.at[me], zrecv.at[me])

    def address(i):
        return (i // 8) * 64 + i % 8

    def send(k):
        n = k // 8
        t, h, w, b = n // 2, n % 2, (k // 2) % 4, k % 2
        dst = ((z + h + 2 * w) % 8) * 8 + ((x + t) % 4) * 2 + (c + b) % 2
        base = dst * SHARE + rep * PART
        for a in range(PADDED // 2):
            i0 = send_ref[base + 2 * a]
            i1 = send_ref[base + min(2 * a + 1, PART - 1)]
            v0 = wide[pl.ds(address(i0), 8, stride=8), :]
            v1 = wide[pl.ds(address(i1), 8, stride=8), :]
            outb[dst, pl.ds(16 * a, 16), :] = jnp.concatenate([v0, v1], axis=0).astype(BF16)

        @pl.when(dst != me)
        def _():
            zcopy(dst).start()

        @pl.when(dst == me)
        def _():
            zlocal().start()

    @pl.loop(0, 16)
    def _(k):
        send(k)

    pl.semaphore_wait(bsem, 3)

    @pl.loop(16, NS)
    def _(k):
        send(k)

    lane1 = lax.broadcasted_iota(jnp.int32, (1, 128), 1)

    def share_of(flat, o):
        a, off = o * SHARE // 128, o * SHARE % 128
        b = min(a + 1, FLAT - 1)
        both = jnp.where(lane1 >= off, flat[a : a + 1, :], flat[b : b + 1, :])
        both = both if off == 0 else pltpu.roll(both, 128 - off, 1)
        return jnp.where(lane1 < SHARE, both, -1)

    for g in range(NG):
        for e in range(8):
            s = ((e // 2) * 2 + g % 2) * 8 + (g // 2) * 2 + e % 2
            ctmp[8 * g + e : 8 * g + e + 1, :] = share_of(place_ref, s)
    block = ctmp[...] // BLK
    ids = jnp.full((NS, 128), -1.0, F32)
    for b in range(table_ref.shape[0] // BLK):
        ids = jnp.where(block == b, (table_ref[b * BLK] - me * 26).astype(F32), ids)
    ordered = ids.astype(BF16)
    lane = lax.broadcasted_iota(jnp.int32, (128, 256), 0)
    spot = lax.broadcasted_iota(jnp.int32, (128, 256), 1)
    keep = (lax.broadcasted_iota(jnp.int32, (NS, 256), 1) % 8) == (
        lax.broadcasted_iota(jnp.int32, (NS, 256), 0) % 8
    )
    for y in range(NR):
        spread = ((lane == PART * y + spot // 8) & (spot < 8 * PART)).astype(F32).astype(BF16)
        ids_y = jnp.dot(ordered, spread, preferred_element_type=F32)
        ids_y = jnp.where(keep, ids_y, 0.0)
        for g in range(NG):
            row = jnp.sum(ids_y[8 * g : 8 * g + 8, :], axis=0, keepdims=True)
            cl[y * NG + g] = jnp.broadcast_to(jnp.where(spot[0:1, :] < 8 * PART, row, -1.0), (8, 256))

    @pl.loop(0, 2 * NG)
    def _(k):
        y = jnp.where(k // NG == 0, y0, y1)
        rows = cl[y * NG + k % NG]
        for h in range(2):
            tile = jnp.broadcast_to(rows[0:1, 128 * h : 128 * h + 128], (128, 128))
            cs[pl.ds(pl.multiple_of(k * 256 + h * 128, 8), 128), :] = tile.T

    ra[...] = jnp.full(ra.shape, -1.0, F32)
    colacc[...] = jnp.full(colacc.shape, -1.0, F32)

    @pl.loop(0, 3 * NG)
    def _(k):
        q[k // NG, k % NG, GROUP:256, :] = jnp.zeros((256 - GROUP, D), BF16)

    sub = lax.broadcasted_iota(jnp.int32, (128, 128), 0)
    for o in range(NS):
        low = share_of(idx_ref, o)
        ctmp[o : o + 1, :] = low
        low = jnp.where(low >= 0, low % 128, -1)
        emb[o // 8, 192:320, 128 * (o % 8) : 128 * (o % 8) + 128] = (sub == low).astype(F32).astype(BF16)

    def group_of(n):
        return ((x - n // 2 + 4) % 4) * 2 + (z + n) % 2

    def ytarget(n):
        return rep_of(pick(3, 0, 3, (n % 2) * 2))

    def ycopy(n, which):
        g = group_of(n)
        at = jnp.where(role >= 2, 1, 0) if which == 0 else 0
        dev = ytarget(n) if which == 0 else rep_of(2)
        return pltpu.make_async_remote_copy(
            src_ref=q.at[0, g, pl.ds(0, GROUP)], dst_ref=q.at[1 + at, g, pl.ds(0, GROUP)],
            send_sem=ysend.at[which, n], recv_sem=yrecv.at[at, n],
            device_id={"rep": dev}, device_id_type=MESH,
        )

    def ywait(n, at):
        g = group_of(n)
        pltpu.make_async_remote_copy(
            src_ref=q.at[0, g, pl.ds(0, GROUP)], dst_ref=q.at[1 + at, g, pl.ds(0, GROUP)],
            send_sem=ysend.at[0, n], recv_sem=yrecv.at[at, n],
            device_id={"rep": ytarget(n)}, device_id_type=MESH,
        ).wait_recv()

    def arrive(n):
        g = group_of(n)
        xs, zs = g // 2, g % 2

        @pl.loop(0, 8)
        def _(e):
            s = ((e // 2) * 2 + zs) * 8 + xs * 2 + e % 2

            @pl.when(s != me)
            def _():
                pltpu.make_async_remote_copy(
                    src_ref=outb.at[s], dst_ref=recv.at[s], send_sem=zsend.at[s], recv_sem=zrecv.at[s],
                    device_id={"shard": s}, device_id_type=MESH,
                ).wait_recv()

            @pl.when(s == me)
            def _():
                zlocal().wait()

            docs = recv[s].astype(F32)
            for i in range(PADDED):
                stage[pl.ds(i * 64 + e, 8, stride=8), :] = docs[8 * i : 8 * i + 8, :]

        @pl.loop(0, GROUP // 16)
        def _(a):
            v = stage[pl.ds(pl.multiple_of(a * 128, 8), 128), :]
            part = []
            for h in range(2):
                tiles = [v[64 * h + 8 * j : 64 * h + 8 * j + 8, :] for j in range(8)]
                square = tiles[0] * tiles[0]
                for j in range(1, 8):
                    square = square + tiles[j] * tiles[j]
                scale = lax.rsqrt(jnp.sum(square, axis=1, keepdims=True) + 1e-06)
                part.append([tile * scale for tile in tiles])
            for j in range(8):
                q[0, g, pl.ds(pl.multiple_of(a * 16, 16), 16), 128 * j : 128 * j + 128] = jnp.concatenate(
                    [part[0][j], part[1][j]], axis=0
                ).astype(BF16)

        @pl.when(role == 1)
        def _():
            ycopy(n, 1).start()

        ycopy(n, 0).start()

    away = lax.broadcasted_iota(jnp.int32, (GROUP, 256), 0) - lax.broadcasted_iota(jnp.int32, (GROUP, 256), 1)

    def tile(pa, ga, pb, gb, diagonal):
        g = lax.dot_general(q[pa, ga, 0:GROUP, :], q[pb, gb], LAST, preferred_element_type=F32)
        yb = jnp.where(pb == 0, y0, jnp.where(pb == 1, y1, y2))
        left = cs[pl.ds(pl.multiple_of((pa * NG + ga) * 256, 8), GROUP), :]
        right = cl[yb * NG + gb]
        at = pl.multiple_of((pa * NG + ga) * GROUP, 8)
        rows = ra[pl.ds(at, GROUP), :]
        for h in range(2):
            same = left.reshape(PADDED, 8, 128) == right[None, :, 128 * h : 128 * h + 128]
            if diagonal is not None:
                away_h = away[:, 128 * h : 128 * h + 128].reshape(PADDED, 8, 128)
                same = same & (away_h != jnp.where(diagonal, 0, 4096))
            vals = jnp.where(same, g[:, 128 * h : 128 * h + 128].reshape(PADDED, 8, 128), -1.0)
            rows = jnp.maximum(rows, vals.reshape(GROUP, 128))
            at_c = pb * NG + gb
            colacc[at_c, :, 128 * h : 128 * h + 128] = jnp.maximum(
                colacc[at_c, :, 128 * h : 128 * h + 128], jnp.max(vals, axis=0)
            )
        ra[pl.ds(at, GROUP), :] = rows

    half = role // 2
    splits = (role == 0) | (role == 2)

    def each(count, score):
        @pl.loop(0, count // 2)
        def _(m):
            score(2 * m)
            score(2 * m + 1)

        @pl.when(count % 2 == 1)
        def _():
            score(count - 1)

    def before(n):
        g = group_of(n)

        @pl.when(role != 1)
        def _():
            other = jnp.where(role == 3, 2 - n % 2, 1)

            def score(m):
                tile(0, g, 0, group_of(m), None)
                tile(0, g, other, group_of(m), None)

            each(n, score)

        @pl.when(role == 1)
        def _():
            @pl.loop(0, n)
            def _(m):
                tile(0, g, 0, group_of(m), None)

        @pl.when(splits)
        def _():
            @pl.loop(0, (n + 1 - half) // 2)
            def _(m):
                tile(0, g, 2, group_of(2 * m + half), None)

        tile(0, g, 0, g, True)

    def after(n):
        g = group_of(n)

        @pl.when(splits)
        def _():
            ywait(n, 0)

            @pl.loop(0, (n + 1 - half) // 2)
            def _(m):
                tile(1, g, 2, group_of(2 * m + half), None)

            @pl.when(n % 2 != half)
            def _():
                @pl.loop(0, n + 1)
                def _(m):
                    tile(0, group_of(m), 1, g, None)

            @pl.when(n % 2 == half)
            def _():
                ywait(n, 1)

                def score(m):
                    gm = group_of(m)
                    tile(0, gm, 1, g, None)
                    tile(0, gm, 2, g, None)
                    tile(1, gm, 2, g, None)

                each(n + 1, score)

        @pl.when(role == 3)
        def _():
            ywait(n, 0)
            ywait(n, 1)

            def score(m):
                gm = group_of(m)
                tile(1, g, 2, gm, None)
                tile(1, gm, 2, g, None)
                tile(0, gm, 2 - m % 2, g, None)

            each(n, score)

            tile(1, g, 2, g, None)
            tile(0, g, 2 - n % 2, g, None)

    @pl.loop(0, NG + 1)
    def _(n):
        @pl.when(n < NG)
        def _():
            arrive(n)

        @pl.when(n > 0)
        def _():
            after(n - 1)

        @pl.when(n < NG)
        def _():
            before(n)

    spot8 = lax.broadcasted_iota(jnp.int32, (8, 256), 1) % 8 == lax.broadcasted_iota(jnp.int32, (8, 256), 0)
    out_lane = lax.broadcasted_iota(jnp.int32, (256, 128), 1) % PART
    gather = (lax.broadcasted_iota(jnp.int32, (256, 128), 0) // 8 == out_lane).astype(F32).astype(BF16)
    lane8 = lax.broadcasted_iota(jnp.int32, (8, 128), 1)
    tsrc[...] = jnp.full(tsrc.shape, -1.0, F32)

    @pl.loop(0, 3)
    def _(p):
        yp = jnp.where(p == 0, y0, jnp.where(p == 1, y1, y2))
        parts = ([], [], [])
        for g in range(NG):
            col = jnp.max(colacc[p * NG + g], axis=0, keepdims=True)
            for part, kept in zip(parts, pieces(col)):
                part.append(jnp.where(spot8, kept, 0.0).astype(BF16).astype(F32))
        best = 0.0
        for part in parts:
            left = jnp.concatenate(part, axis=0).astype(BF16)
            best = best + jnp.dot(left, gather, preferred_element_type=F32)
        mine = lax.broadcasted_iota(jnp.int32, (NS, 128), 1) // PART == yp
        tsrc[...] = jnp.maximum(tsrc[...], jnp.where(mine, best, -1.0))

    @pl.loop(0, 2 * NG)
    def _(k):
        yp = jnp.where(k // NG == 0, y0, y1)
        rows = ra[pl.ds(pl.multiple_of(k * GROUP, 8), GROUP), :].reshape(PADDED, 8, 128)
        rows = jnp.max(rows, axis=2, keepdims=True)
        best = jnp.full((8, 128), -1.0, F32)
        for i in range(PART):
            best = jnp.where(lane8 % PART == i, rows[i], best)
        at = pl.ds(pl.multiple_of((k % NG) * 8, 8), 8)
        tsrc[at, :] = jnp.maximum(tsrc[at, :], jnp.where(lane8 // PART == yp, best, -1.0))

    def r1(k):
        dev = (rep + k) % NR
        return pltpu.make_async_remote_copy(
            src_ref=tsrc.at[pl.ds(pl.multiple_of(dev * 16, 16), 16)], dst_ref=trecv.at[k],
            send_sem=r1send.at[k], recv_sem=r1recv.at[k], device_id={"rep": dev}, device_id_type=MESH,
        )

    for k in range(1, NR):
        r1(k).start()

    @pl.loop(1, NS)
    def _(k):
        zcopy((me + k) % NS).wait_send()

    @pl.loop(0, NG)
    def _(n):
        ycopy(n, 0).wait_send()

        @pl.when(role == 1)
        def _():
            ycopy(n, 1).wait_send()

    for k in range(1, NR):
        r1(k).wait_recv()
    full = tsrc[pl.ds(pl.multiple_of(rep * 16, 16), 16), :]
    full = jnp.maximum(jnp.maximum(full, trecv[1]), jnp.maximum(trecv[2], trecv[3]))
    for r in range(16):
        trow[r] = full[r : r + 1, :]

    def source(r):
        e, g = r % 8, 2 * rep + r // 8
        return ((e // 2) * 2 + g % 2) * 8 + (g // 2) * 2 + e % 2

    def r2(r):
        return pltpu.make_async_remote_copy(
            src_ref=trow.at[r], dst_ref=vrecv.at[me], send_sem=r2send.at[r], recv_sem=r2recv.at[me],
            device_id={"shard": source(r)}, device_id_type=MESH,
        )

    @pl.loop(0, 16)
    def _(r):
        @pl.when(source(r) != me)
        def _():
            r2(r).start()

        @pl.when(source(r) == me)
        def _():
            vrecv[me] = trow[r]

    def r3(k):
        return pltpu.make_async_remote_copy(
            src_ref=res, dst_ref=res, send_sem=r3send.at[k], recv_sem=r3recv,
            device_id={"rep": (rep + k) % NR}, device_id_type=MESH,
        )

    @pl.when(x == rep)
    def _():
        @pl.loop(1, NS)
        def _(k):
            s = (me + k) % NS
            pltpu.make_async_remote_copy(
                src_ref=trow.at[0], dst_ref=vrecv.at[s], send_sem=r2send.at[0], recv_sem=r2recv.at[s],
                device_id={"shard": s}, device_id_type=MESH,
            ).wait_recv()

        sub64 = lax.broadcasted_iota(jnp.int32, (64, 128), 0)
        high = ctmp[...]
        high = jnp.where(high >= 0, high // 128, -1)
        for o in range(NS):
            hit = sub64 == high[o : o + 1, :]
            for w, kept in enumerate(pieces(vrecv[o])):
                emb[o // 8, 64 * w : 64 * w + 64, 128 * (o % 8) : 128 * (o % 8) + 128] = jnp.where(
                    hit, kept, 0.0
                ).astype(BF16)
        done = 0.0
        for j in range(8):
            done = done + lax.dot_general(
                emb[j, 0:192, :], emb[j, 192:320, :], LAST, preferred_element_type=F32
            )
        res[...] = (done[0:64, :] + done[64:128, :] + done[128:192, :])[0:56, :]
        for k in range(1, NR):
            r3(k).start()
        for k in range(1, NR):
            r3(k).wait_send()

    @pl.when(x != rep)
    def _():
        r3(1).wait_recv()

    out_ref[...] = res[0:FLAT, :]

    @pl.loop(0, 16)
    def _(r):
        @pl.when(source(r) != me)
        def _():
            r2(r).wait_send()

    for k in range(1, NR):
        r1(k).wait_send()


def shards(embeddings, send_index, place_index, slot_cluster, pair_list):
    vm = pl.BlockSpec(memory_space=pltpu.VMEM)
    hbm = pl.BlockSpec(memory_space=pl.ANY)
    dma = pltpu.SemaphoreType.DMA
    out = pl.pallas_call(
        kernel,
        out_shape=jax.ShapeDtypeStruct((DOCS // 128, 128), F32),
        in_specs=[hbm] * 5,
        out_specs=vm,
        scratch_shapes=[
            pltpu.SMEM((DOCS,), jnp.int32),
            pltpu.SMEM(slot_cluster.shape, jnp.int32),
            pltpu.VMEM((FLAT, 128), jnp.int32),
            pltpu.VMEM((FLAT, 128), jnp.int32),
            pltpu.VMEM((DOCS * 8, 128), F32),
            pltpu.VMEM((3, NG, 256, D), BF16),
            pltpu.VMEM((NS, MSG, 128), BF16),
            pltpu.VMEM((NS, MSG, 128), BF16),
            pltpu.VMEM((NBUF, CHUNK, D), BF16),
            pltpu.VMEM((GROUP * 8, 128), F32),
            pltpu.VMEM((2 * NG * 256, 128), F32),
            pltpu.VMEM((2 * NG * GROUP, 128), F32),
            pltpu.VMEM((3 * NG, 8, 256), F32),
            pltpu.VMEM((NR * NG, 8, 256), F32),
            pltpu.VMEM((NS, 128), jnp.int32),
            pltpu.VMEM((NS, 128), F32),
            pltpu.VMEM((NR, 16, 128), F32),
            pltpu.VMEM((16, 1, 128), F32),
            pltpu.VMEM((NS, 1, 128), F32),
            pltpu.VMEM((56, 128), F32),
            dma((4,)),
            pltpu.SemaphoreType.REGULAR,
            dma((NBUF,)),
            dma((NS,)),
            dma((NS,)),
            dma((2, NG)),
            dma((2, NG)),
            dma((NR,)),
            dma((NR,)),
            dma((16,)),
            dma((NS,)),
            dma((NR,)),
            dma(()),
        ],
        compiler_params=pltpu.CompilerParams(
            collective_id=0, has_side_effects=True, vmem_limit_bytes=62 * 1024 * 1024
        ),
        name="dedup",
    )(
        send_index, slot_cluster, embeddings, send_index.reshape(FLAT, 128), place_index.reshape(FLAT, 128)
    )
    return out.reshape(-1)


def solution(mesh):
    return jax.shard_map(
        shards,
        mesh=mesh,
        in_specs=(P("shard", None), P("shard"), P("shard"), P("shard"), P(("shard", "rep"), None)),
        out_specs=P("shard"),
        check_vma=False,
    )
```
